512 devices in a mesh: blk: 128 (over x, y_lo, z), grp: 4 (over y_hi, core).
Axes of the slice: x: 4, y: 4 (y_hi: 2, y_lo: 2; y = y_hi * 2 + y_lo), z: 16, core: 2. Of those that a mesh axis runs over, the one named last changes fastest.
Arguments:
- amplitudes: bfloat16 [128, 512, 1024], P('blk', None, 'grp'), may hold values from -6 to 6
- integrals: bfloat16 [1024, 1024, 1024], P('blk', 'grp'), may hold values from -0.1875 to 0.1875
- cd_index: int32 [1024], replicated, may hold values from 0 to 127, as said below
- live_blocks: int32 [128], replicated, may hold values from 4 to 8, as said below
- occ_energy: float32 [512], P('grp'), may hold values from -3 to -0.5
- vir_energy: float32 [128, 1024], P('blk'), may hold values from 0.5 to 4
Outputs:
- amplitude_step: float32 [128, 512, 1024], P('blk', 'grp')
The draws below stay inside these ranges and needn't reach their ends.
Inputs may be any that keep to these rules, and one draw needn't show every extreme that they name: (cd_index[k] - k // 8) mod 128 is at most 2 or at least 126; among the first 4 slots of each pair block every nonzero offset from -2 to 2 occurs once. `live_blocks`: 8 is reached by some pair block in every draw.
All inputs are finite; a program needn't handle non-finite values.
Results may differ from the reference program's by a relative error of at most 0.0003.
Values may be sent and summed in bfloat16 or wider, within the bound.
No kernel may reach another device: no remote copies, remote signals or barrier semaphores. Data moves between devices by JAX's collectives and lax.ppermute only.
A program may use at most 64 MiB of HBM per device.

```python
import jax
import jax.numpy as jnp
from jax import lax

PW = 1024
OCC = 512
INT_DEV = 8
REACH = 2
NPB = 128
NINT = 1024


def draw_cd_index(key, part):
    key_list = jax.random.split(jax.random.fold_in(key, 11), 2)
    shifts = jax.random.randint(key_list[0], (NPB, INT_DEV), -REACH, REACH + 1).astype(jnp.int32)
    rotation = jax.random.randint(key_list[1], (NPB, 1), 0, 2 * REACH).astype(jnp.int32)
    slot_ids = jnp.arange(INT_DEV, dtype=jnp.int32)[None, :]
    cycled = jnp.mod(slot_ids + rotation, 2 * REACH)
    covered = cycled - REACH + (cycled >= REACH).astype(jnp.int32)
    shifts = jnp.where(slot_ids < 2 * REACH, covered, shifts)
    owners = jnp.arange(NPB, dtype=jnp.int32)[:, None]
    return jnp.mod(owners + shifts, NPB).reshape(NINT).astype(jnp.int32)


def draw_live_blocks(key, part):
    key_list = jax.random.split(jax.random.fold_in(key, 23), 3)
    base_live = jax.random.randint(key_list[0], (NPB,), 2 * REACH, 2 * REACH + 2)
    base_live = jnp.minimum(base_live, INT_DEV)
    heavy_rows = jax.random.randint(key_list[1], (NPB,), 0, 8) == 0
    live_counts = jnp.where(heavy_rows, INT_DEV, base_live)
    full_row = jax.random.randint(key_list[2], (), 0, NPB)
    return live_counts.at[full_row].set(INT_DEV).astype(jnp.int32)


def block_levels(stream_key, extent, pieces, least, top_value):
    def one(axis_at, blocks):
        heights = jax.random.uniform(jax.random.fold_in(jax.random.fold_in(stream_key, 6), axis_at), (blocks,), jnp.float32, least / len(pieces), top_value / len(pieces))
        return jnp.repeat(jnp.exp(heights), extent[axis_at] // blocks).reshape((-1,) + (1,) * (len(extent) - axis_at - 1))

    factor_of = one(*pieces[0])
    for cut in pieces[1:]:
        factor_of = factor_of * one(*cut)
    return factor_of


def bell_draw(own_key, extent, width, bound, cuts=(), held_as=jnp.bfloat16):
    array = jax.random.normal(own_key, extent, jnp.float32) * width
    if len(cuts) > 0:
        array = block_levels(own_key, extent, cuts, -0.22, 0.18) * array
    return jnp.clip(array, min=-bound, max=bound).astype(held_as)


def setup_inputs(seed: int = 0) -> dict:
    keys = jax.random.split(jax.random.key(seed), 7)
    return {
        "amplitudes": bell_draw(keys[0], (NPB, OCC, PW), 1.0, 6.0, ((0, 128), (2, 4))),
        "integrals": bell_draw(keys[1], (NINT, PW, PW), PW ** -0.5, 0.1875, ((0, 128), (1, 4))),
        "cd_index": draw_cd_index(jax.random.fold_in(keys[6], 71), 0),
        "live_blocks": draw_live_blocks(jax.random.fold_in(keys[6], 71), 0),
        "occ_energy": jnp.clip(-3.0 + 2.5 * jax.random.uniform(keys[4], (OCC,), jnp.float32) ** block_levels(keys[4], (OCC,), ((0, 4),), -0.2, 0.2), -3.0, -0.5),
        "vir_energy": jnp.clip(0.5 + 3.5 * jax.random.uniform(keys[5], (NPB, PW), jnp.float32) ** block_levels(keys[5], (NPB, PW), ((0, 128),), -0.2, 0.2), 0.5, 4.0),
    }


def reference(amplitudes, integrals, cd_index, live_blocks, occ_energy, vir_energy):
    def one_block(block_index):
        def add_task(running, slot_index):
            task_index = block_index * INT_DEV + slot_index

            def product(running):
                amp_block = amplitudes[cd_index[task_index]]
                return running + jnp.dot(amp_block, integrals[task_index], preferred_element_type=jnp.float32)

            def unchanged(running):
                return running

            return lax.cond(slot_index < live_blocks[block_index], product, unchanged, running), None

        start_sum = jnp.zeros((OCC, PW), jnp.float32)
        ladder, _ = lax.scan(add_task, start_sum, jnp.arange(INT_DEV, dtype=jnp.int32))
        denominator = vir_energy[block_index][None, :] - occ_energy[:, None]
        return ladder / denominator

    return lax.map(one_block, jnp.arange(NPB, dtype=jnp.int32))
```

```python
import functools

import jax
import jax.numpy as jnp
from jax import lax
from jax.experimental import pallas as pl
from jax.experimental.pallas import tpu as pltpu
from jax.sharding import PartitionSpec as P

REACH = 2
LEVELS = 32767.0
LOG_STEPS = 128.0
LEAST_PEAK = 2.0**-120
VMEM_BYTES = 48 * 1024 * 1024

VMEM = pl.BlockSpec(memory_space=pltpu.VMEM)
SMEM = pl.BlockSpec(memory_space=pltpu.SMEM)


def shifted(value, axis, steps):
    count = lax.axis_size(axis)
    pairs = [(source, (source + steps) % count) for source in range(count)]
    return lax.ppermute(value, axis, pairs)


def rows_of(block, height):
    return pl.ds(pl.multiple_of(block * height, height), height)


def row_order(grp):
    high, core = grp // 2, lax.rem(grp, 2)
    return [2 * h + c for c in (core, 1 - core) for h in (high, 1 - high)]


def ladder_kernel(place_ref, cd_ref, live_ref, *refs):
    blocks, (integrals_ref, keep_ref, send_ref, near_ref) = refs[: 2 * REACH + 1], refs[2 * REACH + 1 :]
    here, grp = place_ref[0], place_ref[1]
    slots, depth, width = integrals_ref.shape
    height = keep_ref.shape[0] // 2
    cycle = live_ref.shape[0]
    for at, block in enumerate(row_order(grp)):
        for offset, source in enumerate(blocks):
            near_ref[offset, at * height : (at + 1) * height, :] = source[rows_of(block, height), :]
    keep_ref[...] = jnp.zeros_like(keep_ref)
    send_ref[...] = jnp.zeros_like(send_ref)

    def one_slot(slot, carry):
        offset = lax.rem(cd_ref[here * slots + slot] - here + (REACH + cycle), cycle)
        for half, target in enumerate((keep_ref, send_ref)):
            amp = near_ref[offset, 2 * half * height : 2 * (half + 1) * height, :]
            for column in range(0, width, 256):
                target[:, column : column + 256] += jnp.dot(
                    amp, integrals_ref[slot, :, column : column + 256], preferred_element_type=jnp.float32
                )
        return carry

    lax.fori_loop(0, live_ref[here], one_slot, 0)


def encode_kernel(keep_ref, arrived_ref, code_ref):
    height, width = keep_ref.shape[0] // 2, keep_ref.shape[1]
    marks = []
    for chunk in range(width // 128):
        columns = slice(chunk * 128, (chunk + 1) * 128)
        value = keep_ref[height:, columns] + arrived_ref[height:, columns]
        peak = jnp.maximum(jnp.max(jnp.abs(value), axis=0, keepdims=True), LEAST_PEAK)
        mark = jnp.ceil(jnp.log2(peak) * LOG_STEPS)
        marks.append(mark)
        level = jnp.clip(jnp.round(value * jnp.exp2(mark * (-1.0 / LOG_STEPS)) * LEVELS), -LEVELS, LEVELS)
        code_ref[chunk * height : (chunk + 1) * height, :] = level.astype(jnp.int32).astype(jnp.int16)
    tail = jnp.concatenate(marks + [jnp.zeros_like(marks[0])] * (16 - len(marks)), axis=0)
    code_ref[len(marks) * height :, :] = tail.astype(jnp.int32).astype(jnp.int16)


def finish_kernel(keep_ref, arrived_ref, code_ref, occ_ref, vir_ref, out_ref):
    height, width = out_ref.shape
    chunks = width // 128
    marks = code_ref[chunks * height :, :].astype(jnp.int32).astype(jnp.float32)
    scales = jnp.exp2(marks * (1.0 / LOG_STEPS)) * (1.0 / LEVELS)
    for chunk in range(chunks):
        columns = slice(chunk * 128, (chunk + 1) * 128)
        other = code_ref[chunk * height : (chunk + 1) * height, :].astype(jnp.int32).astype(jnp.float32)
        total = keep_ref[:height, columns] + arrived_ref[:height, columns] + other * scales[chunk : chunk + 1, :]
        out_ref[:, columns] = total / (vir_ref[:, columns] - occ_ref[...])


def call(kernel, out_shape, specs, scratch=(), flops=0):
    return pl.pallas_call(
        kernel,
        out_shape=out_shape,
        in_specs=specs,
        out_specs=jax.tree.map(lambda _: VMEM, out_shape),
        scratch_shapes=scratch,
        compiler_params=pltpu.CompilerParams(vmem_limit_bytes=VMEM_BYTES),
        cost_estimate=pl.CostEstimate(flops=flops, bytes_accessed=4 << 20, transcendentals=0),
    )


def body(amplitudes, integrals, cd_index, live_blocks, occ_energy, vir_energy):
    own = amplitudes[0]
    rows, depth = own.shape
    slots, _, width = integrals.shape
    height = rows // lax.axis_size("grp")
    arrived = {step: shifted(own, "blk", -step) for step in (2, -2, 1, -1)}
    blocks = [arrived[step] if step else own for step in range(-REACH, REACH + 1)]
    place = jnp.stack([lax.axis_index("blk"), lax.axis_index("grp")]).astype(jnp.int32)
    half = jax.ShapeDtypeStruct((2 * height, width), jnp.float32)
    keep, send = call(
        ladder_kernel,
        (half, half),
        [SMEM] * 3 + [VMEM] * (len(blocks) + 1),
        [pltpu.VMEM((len(blocks), rows, depth), own.dtype)],
        2 * slots * rows * depth * width,
    )(place, cd_index, live_blocks, *blocks, integrals)
    other_core = lax.ppermute(send, "grp", [(0, 1), (1, 0), (2, 3), (3, 2)])
    chunks = width // 128
    code = call(encode_kernel, jax.ShapeDtypeStruct((chunks * height + 16, 128), jnp.int16), [VMEM] * 2)(keep, other_core)
    other_chip = lax.ppermute(code, "grp", [(0, 2), (1, 3), (2, 0), (3, 1)])
    out = call(finish_kernel, jax.ShapeDtypeStruct((height, width), jnp.float32), [VMEM] * 5)(
        keep, other_core, other_chip, occ_energy[:, None], vir_energy
    )
    return out[None]


def solution(mesh):
    return jax.shard_map(
        body,
        mesh=mesh,
        in_specs=(P("blk", None, "grp"), P("blk", "grp", None), P(), P(), P("grp"), P("blk", None)),
        out_specs=P("blk", "grp", None),
        check_vma=False,
    )
```

```python
import jax
import jax.numpy as jnp
from jax import lax
from jax.experimental import pallas as pl
from jax.experimental.pallas import tpu as pltpu
from jax.sharding import PartitionSpec as P

REACH = 2
LEVELS = 32767.0
LOG_STEPS = 128.0
LEAST_PEAK = 2.0**-120
VMEM_BYTES = 32 * 1024 * 1024

VMEM = pl.BlockSpec(memory_space=pltpu.VMEM)
SMEM = pl.BlockSpec(memory_space=pltpu.SMEM)
ANY = pl.BlockSpec(memory_space=pl.ANY)
HBM = pl.BlockSpec(memory_space=pltpu.HBM)


def shifted(value, axis, steps):
    count = lax.axis_size(axis)
    pairs = [(source, (source + steps) % count) for source in range(count)]
    return lax.ppermute(value, axis, pairs)


def call(kernel, out_shape, in_specs, out_specs, scratch=(), flops=0, moved=0, aliases={}):
    return pl.pallas_call(
        kernel,
        out_shape=out_shape,
        in_specs=in_specs,
        out_specs=out_specs,
        scratch_shapes=scratch,
        input_output_aliases=aliases,
        compiler_params=pltpu.CompilerParams(vmem_limit_bytes=VMEM_BYTES),
        cost_estimate=pl.CostEstimate(flops=flops, bytes_accessed=moved, transcendentals=0),
    )


def fetch_kernel(cd_hbm, live_hbm, own_hbm, integrals_hbm, plan_ref, own_ref, integrals_ref, cd_ref, live_ref, sems):
    pairs = [(cd_hbm, cd_ref), (live_hbm, live_ref), (own_hbm, own_ref), (integrals_hbm, integrals_ref)]
    copies = [pltpu.make_async_copy(source, target, sems.at[at]) for at, (source, target) in enumerate(pairs)]
    for copy in copies:
        copy.start()
    copies[0].wait()
    copies[1].wait()
    here, grp = lax.axis_index("blk"), lax.axis_index("grp")
    slots, cycle = integrals_ref.shape[0], live_ref.shape[0]
    for slot in range(slots):
        offset = lax.rem(cd_ref[here * slots + slot] - here + (REACH + cycle), cycle)
        plan_ref[slot] = jnp.where(slot < live_ref[here], offset, -1)
    plan_ref[slots] = grp // 2
    plan_ref[slots + 1] = lax.rem(grp, 2)
    copies[2].wait()
    copies[3].wait()


def gated(value, token):
    return call(
        lambda value_ref, token_ref, out_ref: None,
        jax.ShapeDtypeStruct(value.shape, value.dtype),
        [ANY, ANY],
        ANY,
        aliases={0: 0},
    )(value, token)


def ladder_kernel(among, flips, pieces, plan_ref, integrals_ref, *refs):
    count = len(among) * pieces
    sources, rest = refs[:count], refs[count:]
    out_count = len(flips)
    near_ref = rest[-1]
    outs = rest[-1 - out_count : -1]
    starts = rest[: len(rest) - 1 - out_count]
    slots, depth, width = integrals_ref.shape
    height = outs[0].shape[0] // 2
    high, core = plan_ref[slots], plan_ref[slots + 1]
    for which, group in enumerate(flips):
        for at, (flip_high, flip_core) in enumerate(group):
            block_high = 1 - high if flip_high else high
            block_core = 1 - core if flip_core else core
            target = slice((2 * which + at) * height, (2 * which + at + 1) * height)
            for index in range(len(among)):
                if pieces == 1:
                    rows = pl.ds(pl.multiple_of((2 * block_high + block_core) * height, height), height)
                    near_ref[index, target, :] = sources[index][rows, :]
                else:
                    rows = pl.ds(pl.multiple_of(block_core * height, height), height)
                    for piece in range(2):

                        @pl.when(block_high == piece)
                        def _():
                            near_ref[index, target, :] = sources[2 * index + piece][rows, :]

    for which, out in enumerate(outs):
        out[...] = starts[which][...] if starts else jnp.zeros_like(out)

    def one_slot(slot, carry):
        offset = plan_ref[slot]
        index, wanted = jnp.int32(0), offset == among[0]
        for at in range(1, len(among)):
            index = jnp.where(offset == among[at], at, index)
            wanted = wanted | (offset == among[at])

        @pl.when(wanted)
        def _():
            for column in range(0, width, 256):
                matrix = integrals_ref[slot, :, column : column + 256]
                for which, out in enumerate(outs):
                    amp = near_ref[index, 2 * which * height : 2 * (which + 1) * height, :]
                    out[:, column : column + 256] += jnp.dot(amp, matrix, preferred_element_type=jnp.float32)

        return carry

    lax.fori_loop(0, slots, one_slot, 0)


SEND = ((True, True), (False, True))
MINE = ((True, False), (False, False))


def ladder(among, flips, plan, integrals, blocks, starts=(), after=()):
    slots, depth, width = integrals.shape
    pieces = len(blocks) // len(among)
    height = blocks[0].shape[0] * pieces // 4
    row_count = 2 * height * len(flips)
    out = (jax.ShapeDtypeStruct((2 * height, width), jnp.float32),) * len(flips)
    return call(
        lambda *refs: ladder_kernel(among, flips, pieces, *(refs[: len(refs) - 1 - len(flips) - len(after)] + refs[len(refs) - 1 - len(flips) :])),
        out,
        [SMEM] + [VMEM] * (1 + len(blocks) + len(starts)) + [ANY] * len(after),
        (VMEM,) * len(flips),
        [pltpu.VMEM((len(among), row_count, depth), blocks[0].dtype)],
        2 * 3 * row_count * depth * width,
    )(plan, integrals, *blocks, *starts, *after)


def encode_kernel(mine_ref, arrived_ref, code_ref):
    height, width = mine_ref.shape[0] // 2, mine_ref.shape[1]
    marks = []
    for chunk in range(width // 128):
        columns = slice(chunk * 128, (chunk + 1) * 128)
        value = mine_ref[:height, columns] + arrived_ref[:height, columns]
        peak = jnp.maximum(jnp.max(jnp.abs(value), axis=0, keepdims=True), LEAST_PEAK)
        mark = jnp.ceil(jnp.log2(peak) * LOG_STEPS)
        marks.append(mark)
        level = jnp.clip(jnp.round(value * jnp.exp2(mark * (-1.0 / LOG_STEPS)) * LEVELS), -LEVELS, LEVELS)
        code_ref[chunk * height : (chunk + 1) * height, :] = level.astype(jnp.int32).astype(jnp.int16)
    tail = jnp.concatenate(marks + [jnp.zeros_like(marks[0])] * (16 - len(marks)), axis=0)
    code_ref[len(marks) * height :, :] = tail.astype(jnp.int32).astype(jnp.int16)


def finish_kernel(mine_ref, arrived_ref, code_ref, occ_ref, vir_ref, out_ref):
    height, width = out_ref.shape
    chunks = width // 128
    marks = code_ref[chunks * height :, :].astype(jnp.int32).astype(jnp.float32)
    scales = jnp.exp2(marks * (1.0 / LOG_STEPS)) * (1.0 / LEVELS)
    for chunk in range(chunks):
        columns = slice(chunk * 128, (chunk + 1) * 128)
        other = code_ref[chunk * height : (chunk + 1) * height, :].astype(jnp.int32).astype(jnp.float32)
        total = mine_ref[height:, columns] + arrived_ref[height:, columns] + other * scales[chunk : chunk + 1, :]
        out_ref[:, columns] = total / (vir_ref[:, columns] - occ_ref[...])


def to_other_core(value):
    return lax.ppermute(value, "grp", [(0, 1), (1, 0), (2, 3), (3, 2)])


def to_other_chip(value):
    return lax.ppermute(value, "grp", [(0, 2), (1, 3), (2, 0), (3, 1)])


def body(amplitudes, integrals, cd_index, live_blocks, occ_energy, vir_energy):
    own = amplitudes[0]
    height = own.shape[0] // lax.axis_size("grp")
    slots, depth, width = integrals.shape
    arrived = {step: shifted(own, "blk", -step) for step in (1, -1)}
    plan, own_here, integrals_here = call(
        fetch_kernel,
        (
            jax.ShapeDtypeStruct((slots + 2,), jnp.int32),
            jax.ShapeDtypeStruct(own.shape, own.dtype),
            jax.ShapeDtypeStruct(integrals.shape, integrals.dtype),
        ),
        [HBM] * 4,
        (SMEM, VMEM, VMEM),
        [pltpu.SMEM(cd_index.shape, jnp.int32), pltpu.SMEM(live_blocks.shape, jnp.int32), pltpu.SemaphoreType.DMA((4,))],
        0,
        integrals.size * 2,
    )(*[pltpu.with_memory_space_constraint(x, pltpu.HBM) for x in (cd_index, live_blocks, own, integrals)])
    arrived[1] = gated(arrived[1], plan)
    arrived[-1] = gated(arrived[-1], plan)
    arrived[-2] = shifted(arrived[-1], "blk", 1)
    arrived[2] = shifted(arrived[1], "blk", -1)
    blocks = [arrived[step] if step else own_here for step in range(-REACH, REACH + 1)]
    first_send, first_mine = ladder((1, 3, 2), (SEND, MINE), plan, integrals_here, [blocks[at] for at in (1, 3, 2)])
    (send,) = ladder((0, 4), (SEND,), plan, integrals_here, [blocks[at] for at in (0, 4)], (first_send,))
    arrived_core = to_other_core(send)
    (mine,) = ladder((0, 4), (MINE,), plan, integrals_here, [blocks[at] for at in (0, 4)], (first_mine,), (send,))
    chunks = width // 128
    code = call(
        encode_kernel, jax.ShapeDtypeStruct((chunks * height + 16, 128), jnp.int16), [VMEM] * 2, VMEM, (), 0, 1 << 20
    )(mine, arrived_core)
    code_arrived = to_other_chip(code)
    out = call(
        finish_kernel, jax.ShapeDtypeStruct((height, width), jnp.float32), [VMEM] * 5, VMEM, (), 0, 1 << 20
    )(mine, arrived_core, code_arrived, occ_energy[:, None], vir_energy)
    return out[None]


def solution(mesh):
    return jax.shard_map(
        body,
        mesh=mesh,
        in_specs=(P("blk", None, "grp"), P("blk", "grp", None), P(), P(), P("grp"), P("blk", None)),
        out_specs=P("blk", "grp", None),
        check_vma=False,
    )
```

```python
import jax
import jax.numpy as jnp
from jax import lax
from jax.experimental import pallas as pl
from jax.experimental.pallas import tpu as pltpu
from jax.sharding import PartitionSpec as P

REACH = 2
LEVELS = 32767.0
LOG_STEPS = 128.0
LEAST_PEAK = 2.0**-120
VMEM_BYTES = 32 * 1024 * 1024

VMEM = pl.BlockSpec(memory_space=pltpu.VMEM)
SMEM = pl.BlockSpec(memory_space=pltpu.SMEM)
ANY = pl.BlockSpec(memory_space=pl.ANY)
HBM = pl.BlockSpec(memory_space=pltpu.HBM)


def shifted(value, axis, steps):
    count = lax.axis_size(axis)
    pairs = [(source, (source + steps) % count) for source in range(count)]
    return lax.ppermute(value, axis, pairs)


def call(kernel, out_shape, in_specs, out_specs, scratch=(), flops=0, moved=0, aliases={}):
    return pl.pallas_call(
        kernel,
        out_shape=out_shape,
        in_specs=in_specs,
        out_specs=out_specs,
        scratch_shapes=scratch,
        input_output_aliases=aliases,
        compiler_params=pltpu.CompilerParams(vmem_limit_bytes=VMEM_BYTES),
        cost_estimate=pl.CostEstimate(flops=flops, bytes_accessed=moved, transcendentals=0),
    )


def fetch_kernel(cd_hbm, live_hbm, own_hbm, integrals_hbm, plan_ref, own_ref, integrals_ref, cd_ref, live_ref, sems):
    pairs = [(cd_hbm, cd_ref), (live_hbm, live_ref), (own_hbm, own_ref), (integrals_hbm, integrals_ref)]
    copies = [pltpu.make_async_copy(source, target, sems.at[at]) for at, (source, target) in enumerate(pairs)]
    for copy in copies:
        copy.start()
    copies[0].wait()
    copies[1].wait()
    here, grp = lax.axis_index("blk"), lax.axis_index("grp")
    slots, cycle = integrals_ref.shape[0], live_ref.shape[0]
    for slot in range(slots):
        offset = lax.rem(cd_ref[here * slots + slot] - here + (REACH + cycle), cycle)
        plan_ref[slot] = jnp.where(slot < live_ref[here], offset, -1)
    plan_ref[slots] = grp // 2
    plan_ref[slots + 1] = lax.rem(grp, 2)
    copies[2].wait()
    copies[3].wait()


def gated(value, token, flops=0):
    return call(
        lambda value_ref, token_ref, out_ref: None,
        jax.ShapeDtypeStruct(value.shape, value.dtype),
        [ANY, ANY],
        ANY,
        flops=flops,
        aliases={0: 0},
    )(value, token)


def ladder_kernel(among, flips, plan_ref, integrals_ref, *refs):
    sources, rest = refs[: len(among)], refs[len(among) :]
    near_ref = rest[-1]
    outs = rest[-1 - len(flips) : -1]
    starts = rest[: len(rest) - 1 - len(flips)]
    slots, depth, width = integrals_ref.shape
    height = outs[0].shape[0]
    high, core = plan_ref[slots], plan_ref[slots + 1]
    for at, (flip_high, flip_core) in enumerate(flips):
        block = 2 * (1 - high if flip_high else high) + (1 - core if flip_core else core)
        rows = pl.ds(pl.multiple_of(block * height, height), height)
        for index, source in enumerate(sources):
            near_ref[index, at * height : (at + 1) * height, :] = source[rows, :]
        outs[at][...] = starts[at][...] if starts else jnp.zeros_like(outs[at])

    def one_slot(slot, carry):
        offset = plan_ref[slot]
        index, wanted = jnp.int32(0), offset == among[0]
        for at in range(1, len(among)):
            index = jnp.where(offset == among[at], at, index)
            wanted = wanted | (offset == among[at])

        @pl.when(wanted)
        def _():
            for column in range(0, width, 256):
                columns = slice(column, column + 256)
                product = jnp.dot(
                    near_ref[index, :, :], integrals_ref[slot, :, columns], preferred_element_type=jnp.float32
                )
                for at, out in enumerate(outs):
                    out[:, columns] += product[at * height : (at + 1) * height, :]

        return carry

    lax.fori_loop(0, slots, one_slot, 0)


FAR_SEND, FAR_MINE, NEAR_SEND, NEAR_MINE = (True, True), (True, False), (False, True), (False, False)


def ladder(among, flips, plan, integrals, blocks, starts=(), after=()):
    slots, depth, width = integrals.shape
    height = blocks[0].shape[0] // 4
    outs = (jax.ShapeDtypeStruct((height, width), jnp.float32),) * len(flips)
    used = 2 + len(among) + len(starts)
    return call(
        lambda *refs: ladder_kernel(among, flips, *refs[:used], *refs[used + len(after) :]),
        outs,
        [SMEM] + [VMEM] * (used - 1) + [ANY] * len(after),
        (VMEM,) * len(flips),
        [pltpu.VMEM((len(among), height * len(flips), depth), blocks[0].dtype)],
        2 * 3 * height * len(flips) * depth * width,
    )(plan, integrals, *blocks, *starts, *after)


def encode_kernel(mine_ref, arrived_ref, code_ref):
    height, width = mine_ref.shape
    marks = []
    for chunk in range(width // 128):
        columns = slice(chunk * 128, (chunk + 1) * 128)
        value = mine_ref[:, columns] + arrived_ref[:, columns]
        peak = jnp.maximum(jnp.max(jnp.abs(value), axis=0, keepdims=True), LEAST_PEAK)
        mark = jnp.ceil(jnp.log2(peak) * LOG_STEPS)
        marks.append(mark)
        level = jnp.clip(jnp.round(value * jnp.exp2(mark * (-1.0 / LOG_STEPS)) * LEVELS), -LEVELS, LEVELS)
        code_ref[chunk * height : (chunk + 1) * height, :] = level.astype(jnp.int32).astype(jnp.int16)
    tail = jnp.concatenate(marks + [jnp.zeros_like(marks[0])] * (16 - len(marks)), axis=0)
    code_ref[len(marks) * height :, :] = tail.astype(jnp.int32).astype(jnp.int16)


def finish_kernel(mine_ref, arrived_ref, code_ref, occ_ref, vir_ref, out_ref):
    height, width = out_ref.shape
    chunks = width // 128
    marks = code_ref[chunks * height :, :].astype(jnp.int32).astype(jnp.float32)
    scales = jnp.exp2(marks * (1.0 / LOG_STEPS)) * (1.0 / LEVELS)
    for chunk in range(chunks):
        columns = slice(chunk * 128, (chunk + 1) * 128)
        other = code_ref[chunk * height : (chunk + 1) * height, :].astype(jnp.int32).astype(jnp.float32)
        total = mine_ref[:, columns] + arrived_ref[:, columns] + other * scales[chunk : chunk + 1, :]
        out_ref[:, columns] = total / (vir_ref[:, columns] - occ_ref[...])


def to_other_core(value):
    return lax.ppermute(value, "grp", [(0, 1), (1, 0), (2, 3), (3, 2)])


def to_other_chip(value):
    return lax.ppermute(value, "grp", [(0, 2), (1, 3), (2, 0), (3, 1)])


def body(amplitudes, integrals, cd_index, live_blocks, occ_energy, vir_energy):
    own = amplitudes[0]
    height = own.shape[0] // lax.axis_size("grp")
    slots, depth, width = integrals.shape
    arrived = {step: shifted(own, "blk", -step) for step in (1, -1)}
    plan, own_here, integrals_here = call(
        fetch_kernel,
        (
            jax.ShapeDtypeStruct((slots + 2,), jnp.int32),
            jax.ShapeDtypeStruct(own.shape, own.dtype),
            jax.ShapeDtypeStruct(integrals.shape, integrals.dtype),
        ),
        [HBM] * 4,
        (SMEM, VMEM, VMEM),
        [pltpu.SMEM(cd_index.shape, jnp.int32), pltpu.SMEM(live_blocks.shape, jnp.int32), pltpu.SemaphoreType.DMA((4,))],
        0,
        integrals.size * 2,
    )(*[pltpu.with_memory_space_constraint(x, pltpu.HBM) for x in (cd_index, live_blocks, own, integrals)])
    arrived[1] = gated(arrived[1], plan)
    arrived[-1] = gated(arrived[-1], plan)
    arrived[-2] = shifted(arrived[-1], "blk", 1)
    arrived[2] = shifted(arrived[1], "blk", -1)
    blocks = [arrived[step] if step else own_here for step in range(-REACH, REACH + 1)]
    close, distant = (1, 3, 2), (0, 4)
    close_blocks, distant_blocks = [blocks[at] for at in close], [blocks[at] for at in distant]
    first = ladder(
        close, (FAR_SEND, FAR_MINE, NEAR_SEND, NEAR_MINE), plan, integrals_here, close_blocks
    )
    (far_send,) = ladder(distant, (FAR_SEND,), plan, integrals_here, distant_blocks, first[:1])
    far_arrived = to_other_core(far_send)
    (far_mine,) = ladder(distant, (FAR_MINE,), plan, integrals_here, distant_blocks, first[1:2], (far_send,))
    chunks = width // 128
    code = call(
        encode_kernel, jax.ShapeDtypeStruct((chunks * height + 16, 128), jnp.int16), [VMEM] * 2, VMEM, (), 0, 1 << 20
    )(far_mine, far_arrived)
    code_arrived = gated(to_other_chip(code), plan, 4 * 10**9)
    near_send, near_mine = ladder(
        distant, (NEAR_SEND, NEAR_MINE), plan, integrals_here, distant_blocks, first[2:], (code,)
    )
    near_arrived = to_other_core(near_send)
    out = call(
        finish_kernel, jax.ShapeDtypeStruct((height, width), jnp.float32), [VMEM] * 5, VMEM, (), 0, 1 << 20
    )(near_mine, near_arrived, code_arrived, occ_energy[:, None], vir_energy)
    return out[None]


def solution(mesh):
    return jax.shard_map(
        body,
        mesh=mesh,
        in_specs=(P("blk", None, "grp"), P("blk", "grp", None), P(), P(), P("grp"), P("blk", None)),
        out_specs=P("blk", "grp", None),
        check_vma=False,
    )
```

```python
import jax
import jax.numpy as jnp
from jax import lax
from jax.experimental import pallas as pl
from jax.experimental.pallas import tpu as pltpu
from jax.sharding import PartitionSpec as P

REACH = 2
RING = 16
LEVELS = 32767.0
LOG_STEPS = 128.0
LEAST_PEAK = 2.0**-120
VMEM_BYTES = 32 * 1024 * 1024

VMEM = pl.BlockSpec(memory_space=pltpu.VMEM)
SMEM = pl.BlockSpec(memory_space=pltpu.SMEM)
ANY = pl.BlockSpec(memory_space=pl.ANY)
HBM = pl.BlockSpec(memory_space=pltpu.HBM)


def shifted(value, steps, targets=None):
    count = lax.axis_size("blk")
    pairs = [(source, (source + steps) % count) for source in range(count)]
    return lax.ppermute(value, "blk", [pair for pair in pairs if targets is None or pair[1] in targets])


def call(kernel, out_shape, in_specs, out_specs, scratch=(), flops=0, moved=0, aliases={}):
    return pl.pallas_call(
        kernel,
        out_shape=out_shape,
        in_specs=in_specs,
        out_specs=out_specs,
        scratch_shapes=scratch,
        input_output_aliases=aliases,
        compiler_params=pltpu.CompilerParams(vmem_limit_bytes=VMEM_BYTES),
        cost_estimate=pl.CostEstimate(flops=flops, bytes_accessed=moved, transcendentals=0),
    )


def fetch_kernel(cd_hbm, live_hbm, own_hbm, integrals_hbm, plan_ref, own_ref, integrals_ref, cd_ref, live_ref, sems):
    pairs = [(cd_hbm, cd_ref), (live_hbm, live_ref), (own_hbm, own_ref), (integrals_hbm, integrals_ref)]
    copies = [pltpu.make_async_copy(source, target, sems.at[at]) for at, (source, target) in enumerate(pairs)]
    for copy in copies:
        copy.start()
    copies[0].wait()
    copies[1].wait()
    here, grp = lax.axis_index("blk"), lax.axis_index("grp")
    slots, cycle = integrals_ref.shape[0], live_ref.shape[0]
    for slot in range(slots):
        offset = lax.rem(cd_ref[here * slots + slot] - here + (REACH + cycle), cycle)
        plan_ref[slot] = jnp.where(slot < live_ref[here], offset, -1)
    plan_ref[slots] = grp // 2
    plan_ref[slots + 1] = lax.rem(grp, 2)
    plan_ref[slots + 2] = jnp.where(lax.rem(here, RING) == 0, 1, 0)
    copies[2].wait()
    copies[3].wait()


def gated(value, token, flops=0):
    return call(
        lambda value_ref, token_ref, out_ref: None,
        jax.ShapeDtypeStruct(value.shape, value.dtype),
        [ANY, ANY],
        ANY,
        flops=flops,
        aliases={0: 0},
    )(value, token)


def ladder_kernel(among, flips, source_count, plan_ref, integrals_ref, *refs):
    sources, rest = refs[:source_count], refs[source_count:]
    near_ref = rest[-1]
    outs = rest[-1 - len(flips) : -1]
    starts = rest[: len(rest) - 1 - len(flips)]
    slots, depth, width = integrals_ref.shape
    height = outs[0].shape[0]
    high, core, ring_start = plan_ref[slots], plan_ref[slots + 1], plan_ref[slots + 2]
    for at, (flip_high, flip_core) in enumerate(flips):
        block = 2 * (1 - high if flip_high else high) + (1 - core if flip_core else core)
        rows = pl.ds(pl.multiple_of(block * height, height), height)
        target = slice(at * height, (at + 1) * height)
        for index in range(len(among)):
            if source_count == len(among):
                near_ref[index, target, :] = sources[index][rows, :]
                continue
            for which in range(2):

                @pl.when(ring_start == which)
                def _():
                    near_ref[index, target, :] = sources[which * len(among) + index][rows, :]

        outs[at][...] = starts[at][...] if starts else jnp.zeros_like(outs[at])

    def one_slot(slot, carry):
        offset = plan_ref[slot]
        index, wanted = jnp.int32(0), offset == among[0]
        for at in range(1, len(among)):
            index = jnp.where(offset == among[at], at, index)
            wanted = wanted | (offset == among[at])

        @pl.when(wanted)
        def _():
            for column in range(0, width, 256):
                columns = slice(column, column + 256)
                product = jnp.dot(
                    near_ref[index, :, :], integrals_ref[slot, :, columns], preferred_element_type=jnp.float32
                )
                for at, out in enumerate(outs):
                    out[:, columns] += product[at * height : (at + 1) * height, :]

        return carry

    lax.fori_loop(0, slots, one_slot, 0)


FAR_SEND, FAR_MINE, NEAR_SEND, NEAR_MINE = (True, True), (True, False), (False, True), (False, False)


def ladder(among, flips, plan, integrals, blocks, starts=(), after=()):
    slots, depth, width = integrals.shape
    height = blocks[0].shape[0] // 4
    outs = (jax.ShapeDtypeStruct((height, width), jnp.float32),) * len(flips)
    used = 2 + len(blocks) + len(starts)
    return call(
        lambda *refs: ladder_kernel(among, flips, len(blocks), *refs[:used], *refs[used + len(after) :]),
        outs,
        [SMEM] + [VMEM] * (used - 1) + [ANY] * len(after),
        (VMEM,) * len(flips),
        [pltpu.VMEM((len(among), height * len(flips), depth), blocks[0].dtype)],
        2 * 3 * height * len(flips) * depth * width,
    )(plan, integrals, *blocks, *starts, *after)


def encode_kernel(mine_ref, arrived_ref, code_ref):
    height, width = mine_ref.shape
    marks = []
    for chunk in range(width // 128):
        columns = slice(chunk * 128, (chunk + 1) * 128)
        value = mine_ref[:, columns] + arrived_ref[:, columns]
        peak = jnp.maximum(jnp.max(jnp.abs(value), axis=0, keepdims=True), LEAST_PEAK)
        mark = jnp.ceil(jnp.log2(peak) * LOG_STEPS)
        marks.append(mark)
        level = jnp.clip(jnp.round(value * jnp.exp2(mark * (-1.0 / LOG_STEPS)) * LEVELS), -LEVELS, LEVELS)
        code_ref[chunk * height : (chunk + 1) * height, :] = level.astype(jnp.int32).astype(jnp.int16)
    tail = jnp.concatenate(marks + [jnp.zeros_like(marks[0])] * (16 - len(marks)), axis=0)
    code_ref[len(marks) * height :, :] = tail.astype(jnp.int32).astype(jnp.int16)


def finish_kernel(mine_ref, arrived_ref, code_ref, occ_ref, vir_ref, out_hbm, out_ref, sems):
    height, width = out_ref.shape
    chunks, parts = width // 128, sems.shape[0]
    marks = code_ref[chunks * height :, :].astype(jnp.int32).astype(jnp.float32)
    scales = jnp.exp2(marks * (1.0 / LOG_STEPS)) * (1.0 / LEVELS)
    copies = []
    for part in range(parts):
        rows = slice(part * height // parts, (part + 1) * height // parts)
        for chunk in range(chunks):
            columns = slice(chunk * 128, (chunk + 1) * 128)
            coded = slice(chunk * height + rows.start, chunk * height + rows.stop)
            other = code_ref[coded, :].astype(jnp.int32).astype(jnp.float32)
            total = mine_ref[rows, columns] + arrived_ref[rows, columns] + other * scales[chunk : chunk + 1, :]
            out_ref[rows, columns] = total / (vir_ref[:, columns] - occ_ref[rows, :])
        copies.append(pltpu.make_async_copy(out_ref.at[rows, :], out_hbm.at[rows, :], sems.at[part]))
        copies[-1].start()
    for copy in copies:
        copy.wait()


def to_other_core(value):
    return lax.ppermute(value, "grp", [(0, 1), (1, 0), (2, 3), (3, 2)])


def to_other_chip(value):
    return lax.ppermute(value, "grp", [(0, 2), (1, 3), (2, 0), (3, 1)])


def body(amplitudes, integrals, cd_index, live_blocks, occ_energy, vir_energy):
    own = amplitudes[0]
    height = own.shape[0] // lax.axis_size("grp")
    slots, depth, width = integrals.shape
    blocks = range(lax.axis_size("blk"))
    starts_ring = [block for block in blocks if block % RING == 0]
    below, above = shifted(own, 1), shifted(own, -1)
    far_below_start = shifted(own, 2, starts_ring)
    plan, own_here, integrals_here = call(
        fetch_kernel,
        (
            jax.ShapeDtypeStruct((slots + 3,), jnp.int32),
            jax.ShapeDtypeStruct(own.shape, own.dtype),
            jax.ShapeDtypeStruct(integrals.shape, integrals.dtype),
        ),
        [HBM] * 4,
        (SMEM, VMEM, VMEM),
        [pltpu.SMEM(cd_index.shape, jnp.int32), pltpu.SMEM(live_blocks.shape, jnp.int32), pltpu.SemaphoreType.DMA((4,))],
        0,
        integrals.size * 2,
    )(*[pltpu.with_memory_space_constraint(x, pltpu.HBM) for x in (cd_index, live_blocks, own, integrals)])
    below, above = gated(below, plan), gated(above, plan)
    far_below = shifted(below, 1, [block for block in blocks if block % RING])
    far_above = shifted(above, -1)
    close, distant = (1, 3, 2), (0, 4)
    close_blocks = [below, above, own_here]
    distant_blocks = [far_below, far_above, far_below_start, far_above]
    first = ladder(
        close, (FAR_SEND, FAR_MINE, NEAR_SEND, NEAR_MINE), plan, integrals_here, close_blocks
    )
    (far_send,) = ladder(distant, (FAR_SEND,), plan, integrals_here, distant_blocks, first[:1])
    far_arrived = to_other_core(far_send)
    (far_mine,) = ladder(distant, (FAR_MINE,), plan, integrals_here, distant_blocks, first[1:2], (far_send,))
    chunks = width // 128
    code = call(
        encode_kernel, jax.ShapeDtypeStruct((chunks * height + 16, 128), jnp.int16), [VMEM] * 2, VMEM, (), 0, 1 << 20
    )(far_mine, far_arrived)
    code_arrived = gated(to_other_chip(code), plan, 4 * 10**9)
    near_send, near_mine = ladder(
        distant, (NEAR_SEND, NEAR_MINE), plan, integrals_here, distant_blocks, first[2:], (code,)
    )
    near_arrived = to_other_core(near_send)
    out_shape = jax.ShapeDtypeStruct((height, width), jnp.float32)
    out = call(
        finish_kernel,
        out_shape,
        [VMEM] * 5,
        ANY,
        [pltpu.VMEM(out_shape.shape, out_shape.dtype), pltpu.SemaphoreType.DMA((4,))],
        0,
        1 << 20,
    )(near_mine, near_arrived, code_arrived, occ_energy[:, None], vir_energy)
    return out[None]


def solution(mesh):
    return jax.shard_map(
        body,
        mesh=mesh,
        in_specs=(P("blk", None, "grp"), P("blk", "grp", None), P(), P(), P("grp"), P("blk", None)),
        out_specs=P("blk", "grp", None),
        check_vma=False,
    )
```

```python
import jax
import jax.numpy as jnp
from jax import lax
from jax.experimental import pallas as pl
from jax.experimental.pallas import tpu as pltpu
from jax.sharding import PartitionSpec as P

REACH = 2
RING = 16
LEVELS = 32767.0
LOG_STEPS = 128.0
LEAST_PEAK = 2.0**-120
VMEM_BYTES = 32 * 1024 * 1024

VMEM = pl.BlockSpec(memory_space=pltpu.VMEM)
SMEM = pl.BlockSpec(memory_space=pltpu.SMEM)
ANY = pl.BlockSpec(memory_space=pl.ANY)
HBM = pl.BlockSpec(memory_space=pltpu.HBM)


def shifted(value, steps, targets=None):
    count = lax.axis_size("blk")
    pairs = [(source, (source + steps) % count) for source in range(count)]
    return lax.ppermute(value, "blk", [pair for pair in pairs if targets is None or pair[1] in targets])


def call(kernel, out_shape, in_specs, out_specs, scratch=(), flops=0, moved=0, aliases={}):
    return pl.pallas_call(
        kernel,
        out_shape=out_shape,
        in_specs=in_specs,
        out_specs=out_specs,
        scratch_shapes=scratch,
        input_output_aliases=aliases,
        compiler_params=pltpu.CompilerParams(vmem_limit_bytes=VMEM_BYTES),
        cost_estimate=pl.CostEstimate(flops=flops, bytes_accessed=moved, transcendentals=0),
    )


def fetch_kernel(cd_hbm, live_hbm, own_hbm, integrals_hbm, plan_ref, own_ref, integrals_ref, cd_ref, live_ref, sems):
    pairs = [(cd_hbm, cd_ref), (live_hbm, live_ref), (own_hbm, own_ref), (integrals_hbm, integrals_ref)]
    copies = [pltpu.make_async_copy(source, target, sems.at[at]) for at, (source, target) in enumerate(pairs)]
    for copy in copies:
        copy.start()
    copies[0].wait()
    copies[1].wait()
    here, grp = lax.axis_index("blk"), lax.axis_index("grp")
    slots, cycle = integrals_ref.shape[0], live_ref.shape[0]
    for slot in range(slots):
        offset = lax.rem(cd_ref[here * slots + slot] - here + (REACH + cycle), cycle)
        plan_ref[slot] = jnp.where(slot < live_ref[here], offset, -1)
    plan_ref[slots] = grp // 2
    plan_ref[slots + 1] = lax.rem(grp, 2)
    place = lax.rem(here, RING)
    plan_ref[slots + 2] = jnp.where(place == 0, 1, jnp.where((place == RING - 1) & (lax.rem(grp, 2) == 0), 2, 0))
    copies[2].wait()
    copies[3].wait()


def gated(value, token, flops=0):
    return call(
        lambda value_ref, token_ref, out_ref: None,
        jax.ShapeDtypeStruct(value.shape, value.dtype),
        [ANY, ANY],
        ANY,
        flops=flops,
        aliases={0: 0},
    )(value, token)


def ladder_kernel(among, flips, source_count, plan_ref, integrals_ref, *refs):
    sources, rest = refs[:source_count], refs[source_count:]
    near_ref = rest[-1]
    outs = rest[-1 - len(flips) : -1]
    starts = rest[: len(rest) - 1 - len(flips)]
    slots, depth, width = integrals_ref.shape
    height = outs[0].shape[0]
    high, core, edge = plan_ref[slots], plan_ref[slots + 1], plan_ref[slots + 2]
    for at, (flip_high, flip_core) in enumerate(flips):
        block = 2 * (1 - high if flip_high else high) + (1 - core if flip_core else core)
        rows = pl.ds(pl.multiple_of(block * height, height), height)
        target = slice(at * height, (at + 1) * height)
        for index in range(len(among)):
            if source_count == len(among):
                near_ref[index, target, :] = sources[index][rows, :]
                continue
            for which in range(source_count // len(among)):

                @pl.when(edge == which)
                def _():
                    near_ref[index, target, :] = sources[which * len(among) + index][rows, :]

        outs[at][...] = starts[at][...] if starts else jnp.zeros_like(outs[at])

    def one_slot(slot, carry):
        offset = plan_ref[slot]
        index, wanted = jnp.int32(0), offset == among[0]
        for at in range(1, len(among)):
            index = jnp.where(offset == among[at], at, index)
            wanted = wanted | (offset == among[at])

        @pl.when(wanted)
        def _():
            for column in range(0, width, 256):
                columns = slice(column, column + 256)
                product = jnp.dot(
                    near_ref[index, :, :], integrals_ref[slot, :, columns], preferred_element_type=jnp.float32
                )
                for at, out in enumerate(outs):
                    out[:, columns] += product[at * height : (at + 1) * height, :]

        return carry

    lax.fori_loop(0, slots, one_slot, 0)


FAR_SEND, FAR_MINE, NEAR_SEND, NEAR_MINE = (True, True), (True, False), (False, True), (False, False)


def ladder(among, flips, plan, integrals, blocks, starts=(), after=()):
    slots, depth, width = integrals.shape
    height = blocks[0].shape[0] // 4
    outs = (jax.ShapeDtypeStruct((height, width), jnp.float32),) * len(flips)
    used = 2 + len(blocks) + len(starts)
    return call(
        lambda *refs: ladder_kernel(among, flips, len(blocks), *refs[:used], *refs[used + len(after) :]),
        outs,
        [SMEM] + [VMEM] * (used - 1) + [ANY] * len(after),
        (VMEM,) * len(flips),
        [pltpu.VMEM((len(among), height * len(flips), depth), blocks[0].dtype)],
        2 * 3 * height * len(flips) * depth * width,
    )(plan, integrals, *blocks, *starts, *after)


def encode_kernel(mine_ref, arrived_ref, code_ref):
    height, width = mine_ref.shape
    marks = []
    for chunk in range(width // 128):
        columns = slice(chunk * 128, (chunk + 1) * 128)
        value = mine_ref[:, columns] + arrived_ref[:, columns]
        peak = jnp.maximum(jnp.max(jnp.abs(value), axis=0, keepdims=True), LEAST_PEAK)
        mark = jnp.ceil(jnp.log2(peak) * LOG_STEPS)
        marks.append(mark)
        level = jnp.clip(jnp.round(value * jnp.exp2(mark * (-1.0 / LOG_STEPS)) * LEVELS), -LEVELS, LEVELS)
        code_ref[chunk * height : (chunk + 1) * height, :] = level.astype(jnp.int32).astype(jnp.int16)
    tail = jnp.concatenate(marks + [jnp.zeros_like(marks[0])] * (16 - len(marks)), axis=0)
    code_ref[len(marks) * height :, :] = tail.astype(jnp.int32).astype(jnp.int16)


def finish_kernel(mine_ref, arrived_ref, code_ref, occ_ref, vir_ref, out_hbm, out_ref, sems):
    height, width = out_ref.shape
    chunks, parts = width // 128, sems.shape[0]
    marks = code_ref[chunks * height :, :].astype(jnp.int32).astype(jnp.float32)
    scales = jnp.exp2(marks * (1.0 / LOG_STEPS)) * (1.0 / LEVELS)
    copies = []
    for part in range(parts):
        rows = slice(part * height // parts, (part + 1) * height // parts)
        for chunk in range(chunks):
            columns = slice(chunk * 128, (chunk + 1) * 128)
            coded = slice(chunk * height + rows.start, chunk * height + rows.stop)
            other = code_ref[coded, :].astype(jnp.int32).astype(jnp.float32)
            total = mine_ref[rows, columns] + arrived_ref[rows, columns] + other * scales[chunk : chunk + 1, :]
            out_ref[rows, columns] = total / (vir_ref[:, columns] - occ_ref[rows, :])
        copies.append(pltpu.make_async_copy(out_ref.at[rows, :], out_hbm.at[rows, :], sems.at[part]))
        copies[-1].start()
    for copy in copies:
        copy.wait()


def to_other_core(value):
    return lax.ppermute(value, "grp", [(0, 1), (1, 0), (2, 3), (3, 2)])


def to_other_chip(value):
    return lax.ppermute(value, "grp", [(0, 2), (1, 3), (2, 0), (3, 1)])


def body(amplitudes, integrals, cd_index, live_blocks, occ_energy, vir_energy):
    own = amplitudes[0]
    height = own.shape[0] // lax.axis_size("grp")
    slots, depth, width = integrals.shape
    blocks = range(lax.axis_size("blk"))
    below, above = shifted(own, 1), shifted(own, -1)
    far_below_start = shifted(own, 2, [block for block in blocks if block % RING == 0])
    count, group = lax.axis_size("blk"), lax.axis_size("grp")
    over_end = [
        ((block + 2) % count * group + grp, block * group + grp)
        for block in blocks
        for grp in range(group)
        if block % RING == RING - 1 and grp % 2 == 0
    ]
    far_above_end = lax.ppermute(own, ("blk", "grp"), over_end)
    plan, own_here, integrals_here = call(
        fetch_kernel,
        (
            jax.ShapeDtypeStruct((slots + 3,), jnp.int32),
            jax.ShapeDtypeStruct(own.shape, own.dtype),
            jax.ShapeDtypeStruct(integrals.shape, integrals.dtype),
        ),
        [HBM] * 4,
        (SMEM, VMEM, VMEM),
        [pltpu.SMEM(cd_index.shape, jnp.int32), pltpu.SMEM(live_blocks.shape, jnp.int32), pltpu.SemaphoreType.DMA((4,))],
        0,
        integrals.size * 2,
    )(*[pltpu.with_memory_space_constraint(x, pltpu.HBM) for x in (cd_index, live_blocks, own, integrals)])
    far_below = shifted(below, 1, [block for block in blocks if block % RING])
    onward = [
        ((block + 1) % count * group + grp, block * group + grp)
        for block in blocks
        for grp in range(group)
        if block % RING != RING - 1 or grp % 2 != 0
    ]
    far_above = lax.ppermute(above, ("blk", "grp"), onward)
    close, distant = (1, 3, 2), (0, 4)
    close_blocks = [below, above, own_here]
    distant_blocks = [far_below, far_above, far_below_start, far_above, far_below, far_above_end]
    first = ladder(
        close, (FAR_SEND, FAR_MINE, NEAR_SEND, NEAR_MINE), plan, integrals_here, close_blocks
    )
    (far_send,) = ladder(distant, (FAR_SEND,), plan, integrals_here, distant_blocks, first[:1])
    far_arrived = to_other_core(far_send)
    (far_mine,) = ladder(distant, (FAR_MINE,), plan, integrals_here, distant_blocks, first[1:2], (far_send,))
    chunks = width // 128
    code = call(
        encode_kernel, jax.ShapeDtypeStruct((chunks * height + 16, 128), jnp.int16), [VMEM] * 2, VMEM, (), 0, 1 << 20
    )(far_mine, far_arrived)
    code_arrived = gated(to_other_chip(code), plan, 4 * 10**9)
    near_send, near_mine = ladder(
        distant, (NEAR_SEND, NEAR_MINE), plan, integrals_here, distant_blocks, first[2:], (code,)
    )
    near_arrived = to_other_core(near_send)
    out_shape = jax.ShapeDtypeStruct((height, width), jnp.float32)
    out = call(
        finish_kernel,
        out_shape,
        [VMEM] * 5,
        ANY,
        [pltpu.VMEM(out_shape.shape, out_shape.dtype), pltpu.SemaphoreType.DMA((4,))],
        0,
        1 << 20,
    )(near_mine, near_arrived, code_arrived, occ_energy[:, None], vir_energy)
    return out[None]


def solution(mesh):
    return jax.shard_map(
        body,
        mesh=mesh,
        in_specs=(P("blk", None, "grp"), P("blk", "grp", None), P(), P(), P("grp"), P("blk", None)),
        out_specs=P("blk", "grp", None),
        check_vma=False,
    )
```

```python
import jax
import jax.numpy as jnp
from jax import lax
from jax.experimental import pallas as pl
from jax.experimental.pallas import tpu as pltpu
from jax.sharding import PartitionSpec as P

REACH = 2
RING = 16
LEVELS = 32767.0
LOG_STEPS = 128.0
LEAST_PEAK = 2.0**-120
VMEM_BYTES = 32 * 1024 * 1024

VMEM = pl.BlockSpec(memory_space=pltpu.VMEM)
SMEM = pl.BlockSpec(memory_space=pltpu.SMEM)
ANY = pl.BlockSpec(memory_space=pl.ANY)
HBM = pl.BlockSpec(memory_space=pltpu.HBM)


def shifted(value, steps, targets=None):
    count = lax.axis_size("blk")
    pairs = [(source, (source + steps) % count) for source in range(count)]
    return lax.ppermute(value, "blk", [pair for pair in pairs if targets is None or pair[1] in targets])


def call(kernel, out_shape, in_specs, out_specs, scratch=(), flops=0, moved=0, aliases={}):
    return pl.pallas_call(
        kernel,
        out_shape=out_shape,
        in_specs=in_specs,
        out_specs=out_specs,
        scratch_shapes=scratch,
        input_output_aliases=aliases,
        compiler_params=pltpu.CompilerParams(vmem_limit_bytes=VMEM_BYTES),
        cost_estimate=pl.CostEstimate(flops=flops, bytes_accessed=moved, transcendentals=0),
    )


def fetch_kernel(cd_hbm, live_hbm, own_hbm, integrals_hbm, plan_ref, own_ref, integrals_ref, cd_ref, live_ref, sems):
    pairs = [(cd_hbm, cd_ref), (live_hbm, live_ref), (own_hbm, own_ref), (integrals_hbm, integrals_ref)]
    copies = [pltpu.make_async_copy(source, target, sems.at[at]) for at, (source, target) in enumerate(pairs)]
    for copy in copies[:3]:
        copy.start()

    @pl.when(lax.rem(lax.axis_index("grp"), 2) == 1)
    def _():
        copies[3].start()

    copies[0].wait()
    copies[1].wait()
    here, grp = lax.axis_index("blk"), lax.axis_index("grp")
    slots, cycle = integrals_ref.shape[0], live_ref.shape[0]
    for slot in range(slots):
        offset = lax.rem(cd_ref[here * slots + slot] - here + (REACH + cycle), cycle)
        plan_ref[slot] = jnp.where(slot < live_ref[here], offset, -1)
    plan_ref[slots] = grp // 2
    plan_ref[slots + 1] = lax.rem(grp, 2)
    place = lax.rem(here, RING)
    plan_ref[slots + 2] = jnp.where(place == 0, 1, jnp.where((place == RING - 1) & (lax.rem(grp, 2) == 0), 2, 0))
    copies[2].wait()

    @pl.when(lax.rem(lax.axis_index("grp"), 2) == 1)
    def _():
        copies[3].wait()


def fetch_late_kernel(held_ref, integrals_hbm, after_ref, integrals_ref, sem):
    @pl.when(lax.rem(lax.axis_index("grp"), 2) == 0)
    def _():
        copy = pltpu.make_async_copy(integrals_hbm, integrals_ref, sem)
        copy.start()
        copy.wait()


def gated(value, token, flops=0):
    return call(
        lambda value_ref, token_ref, out_ref: None,
        jax.ShapeDtypeStruct(value.shape, value.dtype),
        [ANY, ANY],
        ANY,
        flops=flops,
        aliases={0: 0},
    )(value, token)


def ladder_kernel(among, flips, source_count, plan_ref, integrals_ref, *refs):
    sources, rest = refs[:source_count], refs[source_count:]
    near_ref = rest[-1]
    outs = rest[-1 - len(flips) : -1]
    starts = rest[: len(rest) - 1 - len(flips)]
    slots, depth, width = integrals_ref.shape
    height = outs[0].shape[0]
    high, core, edge = plan_ref[slots], plan_ref[slots + 1], plan_ref[slots + 2]
    for at, (flip_high, flip_core) in enumerate(flips):
        block = 2 * (1 - high if flip_high else high) + (1 - core if flip_core else core)
        rows = pl.ds(pl.multiple_of(block * height, height), height)
        target = slice(at * height, (at + 1) * height)
        for index in range(len(among)):
            if source_count == len(among):
                near_ref[index, target, :] = sources[index][rows, :]
                continue
            for which in range(source_count // len(among)):

                @pl.when(edge == which)
                def _():
                    near_ref[index, target, :] = sources[which * len(among) + index][rows, :]

        outs[at][...] = starts[at][...] if starts else jnp.zeros_like(outs[at])

    def one_slot(slot, carry):
        offset = plan_ref[slot]
        index, wanted = jnp.int32(0), offset == among[0]
        for at in range(1, len(among)):
            index = jnp.where(offset == among[at], at, index)
            wanted = wanted | (offset == among[at])

        @pl.when(wanted)
        def _():
            for column in range(0, width, 256):
                columns = slice(column, column + 256)
                product = jnp.dot(
                    near_ref[index, :, :], integrals_ref[slot, :, columns], preferred_element_type=jnp.float32
                )
                for at, out in enumerate(outs):
                    out[:, columns] += product[at * height : (at + 1) * height, :]

        return carry

    lax.fori_loop(0, slots, one_slot, 0)


FAR_SEND, FAR_MINE, NEAR_SEND, NEAR_MINE = (True, True), (True, False), (False, True), (False, False)


def ladder(among, flips, plan, integrals, blocks, starts=(), after=()):
    slots, depth, width = integrals.shape
    height = blocks[0].shape[0] // 4
    outs = (jax.ShapeDtypeStruct((height, width), jnp.float32),) * len(flips)
    used = 2 + len(blocks) + len(starts)
    return call(
        lambda *refs: ladder_kernel(among, flips, len(blocks), *refs[:used], *refs[used + len(after) :]),
        outs,
        [SMEM] + [VMEM] * (used - 1) + [ANY] * len(after),
        (VMEM,) * len(flips),
        [pltpu.VMEM((len(among), height * len(flips), depth), blocks[0].dtype)],
        2 * 3 * height * len(flips) * depth * width,
    )(plan, integrals, *blocks, *starts, *after)


def encode_kernel(mine_ref, arrived_ref, code_ref):
    height, width = mine_ref.shape
    marks = []
    for chunk in range(width // 128):
        columns = slice(chunk * 128, (chunk + 1) * 128)
        value = mine_ref[:, columns] + arrived_ref[:, columns]
        peak = jnp.maximum(jnp.max(jnp.abs(value), axis=0, keepdims=True), LEAST_PEAK)
        mark = jnp.ceil(jnp.log2(peak) * LOG_STEPS)
        marks.append(mark)
        level = jnp.clip(jnp.round(value * jnp.exp2(mark * (-1.0 / LOG_STEPS)) * LEVELS), -LEVELS, LEVELS)
        code_ref[chunk * height : (chunk + 1) * height, :] = level.astype(jnp.int32).astype(jnp.int16)
    tail = jnp.concatenate(marks + [jnp.zeros_like(marks[0])] * (16 - len(marks)), axis=0)
    code_ref[len(marks) * height :, :] = tail.astype(jnp.int32).astype(jnp.int16)


def finish_kernel(mine_ref, arrived_ref, code_ref, occ_ref, vir_ref, out_hbm, out_ref, sems):
    height, width = out_ref.shape
    chunks, parts = width // 128, sems.shape[0]
    marks = code_ref[chunks * height :, :].astype(jnp.int32).astype(jnp.float32)
    scales = jnp.exp2(marks * (1.0 / LOG_STEPS)) * (1.0 / LEVELS)
    copies = []
    for part in range(parts):
        rows = slice(part * height // parts, (part + 1) * height // parts)
        for chunk in range(chunks):
            columns = slice(chunk * 128, (chunk + 1) * 128)
            coded = slice(chunk * height + rows.start, chunk * height + rows.stop)
            other = code_ref[coded, :].astype(jnp.int32).astype(jnp.float32)
            total = mine_ref[rows, columns] + arrived_ref[rows, columns] + other * scales[chunk : chunk + 1, :]
            out_ref[rows, columns] = total / (vir_ref[:, columns] - occ_ref[rows, :])
        copies.append(pltpu.make_async_copy(out_ref.at[rows, :], out_hbm.at[rows, :], sems.at[part]))
        copies[-1].start()
    for copy in copies:
        copy.wait()


def to_other_core(value):
    return lax.ppermute(value, "grp", [(0, 1), (1, 0), (2, 3), (3, 2)])


def to_other_chip(value):
    return lax.ppermute(value, "grp", [(0, 2), (1, 3), (2, 0), (3, 1)])


def body(amplitudes, integrals, cd_index, live_blocks, occ_energy, vir_energy):
    own = amplitudes[0]
    height = own.shape[0] // lax.axis_size("grp")
    slots, depth, width = integrals.shape
    blocks = range(lax.axis_size("blk"))
    below, above = shifted(own, 1), shifted(own, -1)
    far_below_start = shifted(own, 2, [block for block in blocks if block % RING == 0])
    count, group = lax.axis_size("blk"), lax.axis_size("grp")
    over_end = [
        ((block + 2) % count * group + grp, block * group + grp)
        for block in blocks
        for grp in range(group)
        if block % RING == RING - 1 and grp % 2 == 0
    ]
    far_above_end = lax.ppermute(own, ("blk", "grp"), over_end)
    plan, own_here, integrals_here = call(
        fetch_kernel,
        (
            jax.ShapeDtypeStruct((slots + 3,), jnp.int32),
            jax.ShapeDtypeStruct(own.shape, own.dtype),
            jax.ShapeDtypeStruct(integrals.shape, integrals.dtype),
        ),
        [HBM] * 4,
        (SMEM, VMEM, VMEM),
        [pltpu.SMEM(cd_index.shape, jnp.int32), pltpu.SMEM(live_blocks.shape, jnp.int32), pltpu.SemaphoreType.DMA((4,))],
        0,
        integrals.size * 2,
    )(*[pltpu.with_memory_space_constraint(x, pltpu.HBM) for x in (cd_index, live_blocks, own, integrals)])
    below, above = gated(below, plan), gated(above, plan)
    far_below = shifted(below, 1, [block for block in blocks if block % RING])
    onward = [
        ((block + 1) % count * group + grp, block * group + grp)
        for block in blocks
        for grp in range(group)
        if block % RING != RING - 1 or grp % 2 != 0
    ]
    far_above = lax.ppermute(above, ("blk", "grp"), onward)
    integrals_here = call(
        fetch_late_kernel,
        jax.ShapeDtypeStruct(integrals.shape, integrals.dtype),
        [ANY, HBM, ANY],
        ANY,
        [pltpu.SemaphoreType.DMA],
        0,
        integrals.size * 2,
        {0: 0},
    )(integrals_here, pltpu.with_memory_space_constraint(integrals, pltpu.HBM), plan)
    close, distant = (1, 3, 2), (0, 4)
    close_blocks = [below, above, own_here]
    distant_blocks = [far_below, far_above, far_below_start, far_above, far_below, far_above_end]
    first = ladder(
        close, (FAR_SEND, FAR_MINE, NEAR_SEND, NEAR_MINE), plan, integrals_here, close_blocks
    )
    (far_send,) = ladder(distant, (FAR_SEND,), plan, integrals_here, distant_blocks, first[:1])
    far_arrived = to_other_core(far_send)
    (far_mine,) = ladder(distant, (FAR_MINE,), plan, integrals_here, distant_blocks, first[1:2], (far_send,))
    chunks = width // 128
    code = call(
        encode_kernel, jax.ShapeDtypeStruct((chunks * height + 16, 128), jnp.int16), [VMEM] * 2, VMEM, (), 0, 1 << 20
    )(far_mine, far_arrived)
    code_arrived = gated(to_other_chip(code), plan, 4 * 10**9)
    near_send, near_mine = ladder(
        distant, (NEAR_SEND, NEAR_MINE), plan, integrals_here, distant_blocks, first[2:], (code,)
    )
    near_arrived = to_other_core(near_send)
    out_shape = jax.ShapeDtypeStruct((height, width), jnp.float32)
    out = call(
        finish_kernel,
        out_shape,
        [VMEM] * 5,
        ANY,
        [pltpu.VMEM(out_shape.shape, out_shape.dtype), pltpu.SemaphoreType.DMA((4,))],
        0,
        1 << 20,
    )(near_mine, near_arrived, code_arrived, occ_energy[:, None], vir_energy)
    return out[None]


def solution(mesh):
    return jax.shard_map(
        body,
        mesh=mesh,
        in_specs=(P("blk", None, "grp"), P("blk", "grp", None), P(), P(), P("grp"), P("blk", None)),
        out_specs=P("blk", "grp", None),
        check_vma=False,
    )
```
